128 devices in a mesh: row: 8 (over z, core), col: 16 (over y, x).
Axes of the slice: x: 4, y: 4, z: 4, core: 2. Of those that a mesh axis runs over, the one named last changes fastest.
Arguments:
- front: float32 [24576, 24576], P('row', 'col'), may hold values from -6 to 6
- right_samples: float32 [24576, 256], P('col'), may hold values from -0.0390625 to 0.0390625
- left_samples: float32 [24576, 256], P('row'), may hold values from -0.0390625 to 0.0390625
Outputs:
- row_basis: float32 [24576, 256], P(('col', 'row'))
- row_transfer: float32 [128, 6, 256, 256], P(('col', 'row'))
- col_basis: float32 [24576, 256], P(('row', 'col'))
- col_transfer: float32 [128, 6, 256, 256], P(('row', 'col'))
The draws below stay inside these ranges and needn't reach their ends.
All inputs are finite; a program needn't handle non-finite values.
Results may differ from the reference program's by a relative error of at most 0.00025.
Values sent between devices are 32-bit elements; how exact they have to be, the bound alone decides.
No kernel may reach another device: no remote copies, remote signals or barrier semaphores. Data moves between devices by JAX's collectives and lax.ppermute only.
A program may use at most 128 MiB of HBM per device.

```python
import jax
import jax.numpy as jnp
from jax import lax

MATRIX_ORDER = 24576
SAMPLES = 256
LEVELS = 6
ROW_BLOCK = 24
COL_BLOCK = 12
PIECE_ROWS = 192
N_ROW = 8
N_COL = 16
DEVICES = 128


def shard_levels(key, shape, shards, low, top_value):
    level, own = 1.0, jax.random.fold_in(key, 6)
    for position, blocks in shards:
        draws = jnp.exp(jax.random.uniform(jax.random.fold_in(own, position), (blocks,), jnp.float32, low / len(shards), top_value / len(shards)))
        level = level * jnp.repeat(draws, shape[position] // blocks).reshape([-1 if axis == position else 1 for axis in range(len(shape))])
    return level


def bell_draw(own_key, shape, deviation, reach, cuts=(), dtype=jnp.bfloat16):
    values = deviation * jax.random.normal(own_key, shape, jnp.float32)
    if cuts:
        values = values * shard_levels(own_key, shape, cuts, -0.22, 0.18)
    return jnp.clip(values, -reach, reach).astype(dtype)


def setup_inputs(seed: int = 0) -> dict:
    arg_keys = jax.random.split(jax.random.key(seed), 4)
    return {
        "front": bell_draw(arg_keys[0], (MATRIX_ORDER, MATRIX_ORDER), 1.0, 6.0, ((0, 8), (1, 16)), jnp.float32),
        "right_samples": bell_draw(arg_keys[1], (MATRIX_ORDER, SAMPLES), MATRIX_ORDER ** -0.5, 0.0390625, ((0, 16),), jnp.float32),
        "left_samples": bell_draw(arg_keys[2], (MATRIX_ORDER, SAMPLES), MATRIX_ORDER ** -0.5, 0.0390625, ((0, 8),), jnp.float32),
    }


def build_tree(sample):
    highest = lax.Precision.HIGHEST
    pieces = sample.reshape(DEVICES, PIECE_ROWS, SAMPLES)
    grams = jnp.einsum('pls,plt->pst', pieces, pieces, precision=highest)
    factors = []
    nodes = grams
    for level in range(LEVELS + 1):
        nodes = nodes.reshape(-1, 2, SAMPLES, SAMPLES).sum(axis=1)
        factors.append(jnp.linalg.cholesky(nodes))
    leaves = jnp.repeat(factors[0], 2, axis=0)

    def leaf_basis(factor, piece):
        return jax.scipy.linalg.solve_triangular(factor, piece.T, lower=True).T
    basis = jax.vmap(leaf_basis)(leaves, pieces).reshape(MATRIX_ORDER, SAMPLES)

    def transfer(parent, child):
        return jax.scipy.linalg.solve_triangular(parent, child, lower=True).T
    levels = []
    for level in range(LEVELS):
        child = jnp.repeat(factors[level], 2 ** (level + 1), axis=0)
        parent = jnp.repeat(factors[level + 1], 2 ** (level + 2), axis=0)
        levels.append(jax.vmap(transfer)(parent, child))
    return (basis, jnp.stack(levels, axis=1))

def reference(front, right_samples, left_samples):
    highest = lax.Precision.HIGHEST
    stored_sample = jnp.dot(front.astype(jnp.float32), right_samples.astype(jnp.float32), precision=highest, preferred_element_type=jnp.float32)
    stored_cosample = lax.dot_general(front.astype(jnp.float32), left_samples.astype(jnp.float32), (((0,), (0,)), ((), ())), precision=highest, preferred_element_type=jnp.float32)
    row_sample = stored_sample.reshape(N_ROW, N_ROW * N_COL, ROW_BLOCK, SAMPLES).transpose(1, 0, 2, 3).reshape(MATRIX_ORDER, SAMPLES)
    col_sample = stored_cosample.reshape(N_COL, N_COL * N_ROW, COL_BLOCK, SAMPLES).transpose(1, 0, 2, 3).reshape(MATRIX_ORDER, SAMPLES)
    row_basis, row_transfer = build_tree(row_sample)
    col_basis, col_transfer = build_tree(col_sample)
    return (row_basis, row_transfer, col_basis, col_transfer)
```

```python
import jax
import jax.numpy as jnp
from jax import lax
from jax.experimental import pallas as pl
from jax.experimental.pallas import tpu as pltpu
from jax.sharding import PartitionSpec as P

WIDTH = 256
BLOCK = 64
HALF = 128
HIGHEST = lax.Precision.HIGHEST


def mm(a, b, ca, cb):
    return lax.dot_general(
        a, b, (((ca,), (cb,)), ((), ())), precision=HIGHEST, preferred_element_type=jnp.float32
    )


def factor_blocks(blocks, lower_out, upper_out):
    lanes = blocks.shape[1]
    sub = lax.broadcasted_iota(jnp.int32, (8, HALF), 0)
    lane = lax.broadcasted_iota(jnp.int32, (8, HALF), 1)
    seg = lane & (BLOCK - 1)
    base = lane - seg
    tiles = BLOCK // 8
    groups = lanes // HALF
    state = [
        [blocks[8 * t : 8 * t + 8, HALF * c : HALF * (c + 1)] for c in range(groups)]
        for t in range(tiles)
    ]
    for k in range(BLOCK):
        top, inner = k // 8, k % 8
        at = seg == k
        for c in range(groups):
            row = state[top][c][inner : inner + 1, :]
            column = {
                t: jnp.take_along_axis(state[t][c], base + k, axis=1, mode="promise_in_bounds")
                for t in range(top, tiles)
            }
            pivot = column[top][inner : inner + 1, :]
            scale = lax.rsqrt(pivot)
            scale = scale * (1.5 - 0.5 * pivot * scale * scale)
            done = jnp.where(at[:1], 1.0, row) * scale
            place = slice(HALF * c, HALF * (c + 1))
            lower_out[k : k + 1, place] = jnp.where(seg[:1] <= k, done, 0.0)
            upper_out[k : k + 1, place] = jnp.where(
                seg[:1] > k, done, jnp.where(at[:1], pivot * scale, 0.0)
            )
            scaled = done * scale
            for t in range(top, tiles):
                if t == top and inner == 7:
                    continue
                new = jnp.where(at, 0.0, state[t][c]) - column[t] * scaled
                state[t][c] = jnp.where(sub > inner, new, state[t][c]) if t == top else new


def factor_nodes(source, work, upper, inverse, blocks, lower_out, upper_out):
    count = source.shape[0]
    column = lax.broadcasted_iota(jnp.int32, (BLOCK, WIDTH), 1)
    for j in range(WIDTH // BLOCK):
        src = source if j == 0 else work
        lo, hi = j * BLOCK, (j + 1) * BLOCK
        for b in range(count):
            blocks[:, b * BLOCK : (b + 1) * BLOCK] = src[b, lo:hi, lo:hi]
        factor_blocks(blocks, lower_out, upper_out)
        inside = (column >= lo) & (column < hi)
        for b in range(count):
            inv = lower_out[:, b * BLOCK : (b + 1) * BLOCK]
            rows = mm(inv, jnp.where(inside, 0.0, src[b, lo:hi, :]), 1, 0)
            upper[b, lo:hi, :] = jnp.where(column >= hi, rows, 0.0)
            inverse[b, lo:hi, :] = jnp.where(column < lo, rows, 0.0)
            upper[b, lo:hi, lo:hi] = upper_out[:, b * BLOCK : (b + 1) * BLOCK]
            inverse[b, lo:hi, lo:hi] = inv
            if hi < WIDTH:
                panel = mm(src[b, hi:, lo:hi], inv, 1, 1)
                work[b, hi:, :] = src[b, hi:, :] - mm(panel, rows, 1, 0)
                work[b, hi:, lo:hi] = -mm(panel, inv, 1, 0)


def unpack(packed, full):
    for b in range(packed.shape[0]):
        mixed = packed[b, HALF : 2 * HALF, :]
        turned = mixed.T
        row = lax.broadcasted_iota(jnp.int32, (HALF, HALF), 0)
        col = lax.broadcasted_iota(jnp.int32, (HALF, HALF), 1)
        across = packed[b, :HALF, :]
        full[b, :HALF, HALF:] = across
        full[b, HALF:, :HALF] = across.T
        full[b, :HALF, :HALF] = jnp.where(row >= col, mixed, turned)
        diagonal = jnp.broadcast_to(packed[b, 2 * HALF : 2 * HALF + 1, :], (HALF, HALF))
        full[b, HALF:, HALF:] = jnp.where(
            row == col, diagonal, jnp.where(row < col, mixed, turned)
        )


def tree_kernel(
    row_piece, col_piece, packed, row_basis, row_transfer, col_basis, col_transfer,
    full, work, upper, inverse, blocks, lower_out, upper_out,
):
    unpack(packed, full)
    factor_nodes(full, work, upper, inverse, blocks, lower_out, upper_out)
    half = packed.shape[0] // 2
    row_basis[...] = mm(row_piece[...], inverse[0], 1, 1)
    col_basis[...] = mm(col_piece[...], inverse[half], 1, 1)
    for t in range(half - 1):
        row_transfer[t] = mm(upper[t], inverse[t + 1], 1, 1)
        col_transfer[t] = mm(upper[half + t], inverse[half + t + 1], 1, 1)


def finish_trees(row_piece, col_piece, packed):
    count = packed.shape[0]
    basis = jax.ShapeDtypeStruct(row_piece.shape, jnp.float32)
    transfer = jax.ShapeDtypeStruct((count // 2 - 1, WIDTH, WIDTH), jnp.float32)
    vmem = pl.BlockSpec(memory_space=pltpu.VMEM)
    return pl.pallas_call(
        tree_kernel,
        out_shape=[basis, transfer, basis, transfer],
        in_specs=[vmem] * 3,
        out_specs=[vmem] * 4,
        scratch_shapes=[pltpu.VMEM((count, WIDTH, WIDTH), jnp.float32)] * 4
        + [pltpu.VMEM((BLOCK, count * BLOCK), jnp.float32)] * 3,
        compiler_params=pltpu.CompilerParams(vmem_limit_bytes=48 << 20),
    )(row_piece, col_piece, packed)


def pack(gram):
    first, last = gram[:HALF, :HALF], gram[HALF:, HALF:]
    row = lax.broadcasted_iota(jnp.int32, (HALF, HALF), 0)
    col = lax.broadcasted_iota(jnp.int32, (HALF, HALF), 1)
    diagonal = jnp.sum(jnp.where(row == col, last, 0.0), axis=0, keepdims=True)
    return jnp.concatenate(
        [gram[:HALF, HALF:], jnp.where(row >= col, first, last), jnp.broadcast_to(diagonal, (8, HALF))],
        axis=0,
    )


def route_core():
    return ("row", [(r, r ^ 1) for r in range(8)])


def route_z(move):
    return ("row", [(z * 2 + k, move(z) * 2 + k) for z in range(4) for k in range(2)])


def route_x(move):
    return ("col", [(y * 4 + x, y * 4 + move(x)) for y in range(4) for x in range(4)])


def route_y(move):
    return ("col", [(y * 4 + x, move(y) * 4 + x) for y in range(4) for x in range(4)])


def send(array, route):
    return lax.ppermute(array, route[0], route[1])


def scatter_sum(parts, place, route_of, axis):
    pick = lambda shift: lax.dynamic_index_in_dim(parts, (place + shift) & 3, axis, keepdims=False)
    arrived = [
        send(pick(shift), route_of(lambda p, shift=shift: (p + shift) & 3)) for shift in (1, 3, 2)
    ]
    return pick(0) + arrived[0] + arrived[1] + arrived[2]


def quad_levels(gram, route_of):
    one, three, two = (send(gram, route_of(lambda p, bit=bit: p ^ bit)) for bit in (1, 3, 2))
    pair = gram + one
    return pair, pair + (two + three)


def per_device(front, right_samples, left_samples):
    row_at, col_at = lax.axis_index("row"), lax.axis_index("col")
    core_at, z_at, x_at, y_at = row_at & 1, row_at >> 1, col_at & 3, col_at >> 2
    width = right_samples.shape[1]

    partial = mm(front, right_samples, 1, 0).reshape(4, 4, 2, 96, width)
    first = scatter_sum(partial[:, :, 0], x_at, route_x, 1)
    second = scatter_sum(partial[:, :, 1], y_at, route_y, 0)
    owned_rows = jnp.concatenate(
        [scatter_sum(first, y_at, route_y, 0), scatter_sum(second, x_at, route_x, 0)], axis=0
    )
    copartial = mm(front, left_samples, 0, 0).reshape(4, 2, 192, width)
    mine = lax.dynamic_index_in_dim(copartial, core_at, 1, keepdims=False)
    other = lax.dynamic_index_in_dim(copartial, 1 - core_at, 1, keepdims=False)
    owned_cols = scatter_sum(mine + send(other, route_core()), z_at, route_z, 0)

    row_piece = lax.all_to_all(owned_rows, "row", split_axis=0, concat_axis=0, tiled=True)
    col_piece = lax.all_to_all(owned_cols, "col", split_axis=0, concat_axis=0, tiled=True)

    gram = pack(mm(row_piece, row_piece, 0, 0))
    nodes = [gram + send(gram, route_core())]
    for route_of in (route_z, route_x, route_y):
        nodes += quad_levels(nodes[-1], route_of)
    gram = pack(mm(col_piece, col_piece, 0, 0))
    conodes = list(quad_levels(gram, route_x))
    conodes += quad_levels(conodes[-1], route_y)
    conodes.append(conodes[-1] + send(conodes[-1], route_core()))
    conodes += quad_levels(conodes[-1], route_z)

    row_basis, row_transfer, col_basis, col_transfer = finish_trees(
        row_piece, col_piece, jnp.stack(nodes + conodes, axis=0)
    )
    return row_basis, row_transfer[None], col_basis, col_transfer[None]


def solution(mesh):
    in_specs = (P("row", "col"), P("col", None), P("row", None))
    out_specs = (
        P(("col", "row"), None),
        P(("col", "row"), None, None, None),
        P(("row", "col"), None),
        P(("row", "col"), None, None, None),
    )
    return jax.shard_map(
        per_device, mesh=mesh, in_specs=in_specs, out_specs=out_specs, check_vma=False
    )
```

```python
import functools

import jax
import jax.numpy as jnp
from jax import lax
from jax.experimental import pallas as pl
from jax.experimental.pallas import tpu as pltpu
from jax.sharding import PartitionSpec as P

WIDTH = 256
BLOCK = 64
HALF = 128
AHEAD = 2
BF = jnp.bfloat16


def dot(a, b, ca, cb, precision=None):
    return lax.dot_general(
        a, b, (((ca,), (cb,)), ((), ())), precision=precision, preferred_element_type=jnp.float32
    )


def split2(x):
    first = x.astype(BF)
    return first, (x - first.astype(jnp.float32)).astype(BF)


def split3(x):
    first = x.astype(BF)
    rest = x - first.astype(jnp.float32)
    second = rest.astype(BF)
    return first, second, (rest - second.astype(jnp.float32)).astype(BF)


def left6(parts, axis):
    a, b, c = parts
    return jnp.concatenate([a, a, a], axis=axis), jnp.concatenate([b, b, c], axis=axis)


def right6(parts, axis):
    a, b, c = parts
    return jnp.concatenate([a, b, c], axis=axis), jnp.concatenate([a, b, a], axis=axis)


def dot6(left, right, ca, cb):
    return dot(left[0], right[0], ca, cb) + dot(left[1], right[1], ca, cb)


def dot3(a, b, ca, cb):
    return dot(a[0], b[0], ca, cb) + (dot(a[0], b[1], ca, cb) + dot(a[1], b[0], ca, cb))


def row_kernel(place, f0, f1, f2, f3, samples, *refs):
    outs_x, outs_y = refs[:4], refs[4:8]
    coarse, fine, high, low = refs[8:]
    step = pl.program_id(0)

    @pl.when(step == 0)
    def _():
        coarse[...], fine[...] = split2(samples[...])

    for d, block in enumerate((f0, f1, f2, f3)):
        high[192 * d : 192 * (d + 1), :], low[192 * d : 192 * (d + 1), :] = split2(block[...])
    total = dot3((high[...], low[...]), (coarse[...], fine[...]), 1, 0)
    for d in range(4):
        outs_y[d][step] = total[192 * d + 96 : 192 * d + 192]

        @pl.when(step == d)
        def _(d=d):
            for e in range(4):
                outs_x[d][e] = total[192 * e : 192 * e + 96]


def row_product(front, samples, place):
    depth = front.shape[1]
    slab = jax.ShapeDtypeStruct((4, 96, WIDTH), jnp.float32)

    def block(d):
        return pl.BlockSpec(
            (192, depth), lambda i, place: (4 * ((place[0] + d) & 3) + ((place[1] + i) & 3), 0)
        )

    def whole(shape):
        return pl.BlockSpec(shape, lambda i, place: (0,) * len(shape))

    outs = pl.pallas_call(
        row_kernel,
        out_shape=[slab] * 8,
        grid_spec=pltpu.PrefetchScalarGridSpec(
            num_scalar_prefetch=1,
            grid=(4,),
            in_specs=[block(d) for d in range(4)] + [whole((depth, WIDTH))],
            out_specs=[whole(slab.shape)] * 8,
            scratch_shapes=[pltpu.VMEM((depth, WIDTH), BF)] * 2 + [pltpu.VMEM((768, depth), BF)] * 2,
        ),
        compiler_params=pltpu.CompilerParams(vmem_limit_bytes=40 << 20),
    )(place, front, front, front, front, samples)
    return outs[:4], outs[4:]


def col_kernel(place, front, samples, mine, other, total):
    step = pl.program_id(0)
    part = dot3(split2(front[...]), split2(samples[...]), 0, 0)

    @pl.when(step == 0)
    def _():
        total[...] = part

    @pl.when(step > 0)
    def _():
        total[...] += part

    @pl.when(step == pl.num_programs(0) - 1)
    def _():
        for d in range(4):
            base = 2 * ((place[2] + d) & 3)
            mine[d] = total[pl.ds(pl.multiple_of(192 * (base + place[3]), 192), 192), :]
            other[d] = total[pl.ds(pl.multiple_of(192 * (base + 1 - place[3]), 192), 192), :]


def col_product(front, samples, place):
    rows, depth = 768, front.shape[1]
    slab = jax.ShapeDtypeStruct((4, 192, WIDTH), jnp.float32)

    def whole(shape):
        return pl.BlockSpec(shape, lambda i, place: (0,) * len(shape))

    return pl.pallas_call(
        col_kernel,
        out_shape=[slab] * 2,
        grid_spec=pltpu.PrefetchScalarGridSpec(
            num_scalar_prefetch=1,
            grid=(front.shape[0] // rows,),
            in_specs=[
                pl.BlockSpec((rows, depth), lambda i, place: (i, 0)),
                pl.BlockSpec((rows, WIDTH), lambda i, place: (i, 0)),
            ],
            out_specs=[whole(slab.shape)] * 2,
            scratch_shapes=[pltpu.VMEM((depth, WIDTH), jnp.float32)],
        ),
        compiler_params=pltpu.CompilerParams(vmem_limit_bytes=40 << 20),
        cost_estimate=pl.CostEstimate(
            flops=6 * front.size * WIDTH, bytes_accessed=4 * front.size, transcendentals=0
        ),
    )(place, front, samples)


def gram_kernel(piece, packed):
    gram = dot(piece[...], piece[...], 0, 0, lax.Precision.HIGHEST)
    row = lax.broadcasted_iota(jnp.int32, (HALF, HALF), 0)
    col = lax.broadcasted_iota(jnp.int32, (HALF, HALF), 1)
    last = gram[HALF:, HALF:]
    packed[:HALF, :] = gram[:HALF, HALF:]
    packed[HALF:WIDTH, :] = jnp.where(row >= col, gram[:HALF, :HALF], last)
    diagonal = jnp.sum(jnp.where(row == col, last, 0.0), axis=0, keepdims=True)
    packed[WIDTH:, :] = jnp.broadcast_to(diagonal, (8, HALF))


def packed_gram(piece):
    vmem = pl.BlockSpec(memory_space=pltpu.VMEM)
    return pl.pallas_call(
        gram_kernel,
        out_shape=jax.ShapeDtypeStruct((WIDTH + 8, HALF), jnp.float32),
        in_specs=[vmem],
        out_specs=vmem,
    )(piece)


def unpack(packed, full):
    row = lax.broadcasted_iota(jnp.int32, (HALF, HALF), 0)
    col = lax.broadcasted_iota(jnp.int32, (HALF, HALF), 1)
    for b, source in enumerate(packed):
        mixed, across = source[HALF:WIDTH, :], source[:HALF, :]
        turned = mixed.T
        full[b, :HALF, HALF:] = across
        full[b, HALF:, :HALF] = across.T
        full[b, :HALF, :HALF] = jnp.where(row >= col, mixed, turned)
        diagonal = jnp.broadcast_to(source[WIDTH : WIDTH + 1, :], (HALF, HALF))
        full[b, HALF:, HALF:] = jnp.where(
            row == col, diagonal, jnp.where(row < col, mixed, turned)
        )


def factor_blocks(blocks, lower_out, upper_out):
    lanes = blocks.shape[1]
    sub = lax.broadcasted_iota(jnp.int32, (8, HALF), 0)
    lane = lax.broadcasted_iota(jnp.int32, (8, HALF), 1)
    seg = lane & (BLOCK - 1)
    base = lane - seg
    tiles = BLOCK // 8
    groups = lanes // HALF
    state = [
        [blocks[8 * t : 8 * t + 8, HALF * c : HALF * (c + 1)] for c in range(groups)]
        for t in range(tiles)
    ]

    def spread(c, k):
        return {
            t: jnp.take_along_axis(state[t][c], base + k, axis=1, mode="promise_in_bounds")
            for t in range(k // 8, tiles)
        }

    ahead = [{k: spread(c, k) for k in range(AHEAD)} for c in range(groups)]
    for k in range(BLOCK):
        top, inner = k // 8, k % 8
        at = seg == k
        for c in range(groups):
            row = state[top][c][inner : inner + 1, :]
            if k + AHEAD < BLOCK:
                ahead[c][k + AHEAD] = spread(c, k + AHEAD)
            column = ahead[c].pop(k)
            pivot = column[top][inner : inner + 1, :]
            scale = lax.rsqrt(pivot)
            square = scale * scale
            for m, later in ahead[c].items():
                weight = column[m // 8][m % 8 : m % 8 + 1, :] * square
                ahead[c][m] = {t: later[t] - column[t] * weight for t in later}
            done = jnp.where(at[:1], 1.0, row) * scale
            place = slice(HALF * c, HALF * (c + 1))
            lower_out[k : k + 1, place] = jnp.where(seg[:1] <= k, done, 0.0)
            upper_out[k : k + 1, place] = jnp.where(
                seg[:1] > k, done, jnp.where(at[:1], pivot * scale, 0.0)
            )
            scaled = done * scale
            for t in range(top, tiles):
                if t == top and inner == 7:
                    continue
                new = jnp.where(at, 0.0, state[t][c]) - column[t] * scaled
                state[t][c] = jnp.where(sub > inner, new, state[t][c]) if t == top else new


def factor_nodes(source, work, upper, inverse, blocks, lower_out, upper_out):
    count = source.shape[0]
    column = lax.broadcasted_iota(jnp.int32, (BLOCK, WIDTH), 1)
    row = lax.broadcasted_iota(jnp.int32, (BLOCK, WIDTH), 0)
    columns = lax.broadcasted_iota(jnp.int32, (WIDTH, WIDTH), 1)
    for j in range(WIDTH // BLOCK):
        src = source if j == 0 else work
        lo, hi = j * BLOCK, (j + 1) * BLOCK
        for b in range(count):
            blocks[:, b * BLOCK : (b + 1) * BLOCK] = src[b, lo:hi, lo:hi]
        factor_blocks(blocks, lower_out, upper_out)
        inside = (column >= lo) & (column < hi)
        unit = jnp.where(column - lo == row, 1.0, 0.0)
        for b in range(count):
            inv = lower_out[:, b * BLOCK : (b + 1) * BLOCK]
            line = jnp.where(inside, unit, src[b, lo:hi, :])
            rows = dot6(left6(split3(inv), 1), right6(split3(line), 0), 1, 0)
            upper[b, lo:hi, :] = jnp.where(column >= hi, rows, 0.0)
            inverse[b, lo:hi, :] = jnp.where(column < hi, rows, 0.0)
            upper[b, lo:hi, lo:hi] = upper_out[:, b * BLOCK : (b + 1) * BLOCK]
            if hi < WIDTH:
                parts = split3(rows)
                panel = tuple(p[:, hi:] for p in parts)
                change = dot6(left6(panel, 0), right6(parts, 0), 0, 0)
                c = columns[hi:]
                kept = jnp.where((c >= lo) & (c < hi), 0.0, src[b, hi:, :])
                work[b, hi:, :] = kept - change


def tree_kernel(*refs, count):
    pieces, packed, outs = refs[:2], refs[2 : 2 + count], refs[2 + count : 6 + count]
    full, work, upper, inverse, blocks, lower_out, upper_out = refs[6 + count :]
    unpack(packed, full)
    factor_nodes(full, work, upper, inverse, blocks, lower_out, upper_out)
    levels = count // 2
    for side in range(2):
        basis, transfer = outs[2 * side : 2 * side + 2]
        leaf = side * levels
        basis[...] = dot3(split2(pieces[side][...]), split2(inverse[leaf]), 1, 1)
        for t in range(levels - 1):
            transfer[t] = dot3(split2(upper[leaf + t]), split2(inverse[leaf + t + 1]), 1, 1)


def finish_trees(row_piece, col_piece, packed):
    count = len(packed)
    basis = jax.ShapeDtypeStruct(row_piece.shape, jnp.float32)
    transfer = jax.ShapeDtypeStruct((count // 2 - 1, WIDTH, WIDTH), jnp.float32)
    vmem = pl.BlockSpec(memory_space=pltpu.VMEM)
    return pl.pallas_call(
        functools.partial(tree_kernel, count=count),
        out_shape=[basis, transfer, basis, transfer],
        in_specs=[vmem] * (2 + count),
        out_specs=[vmem] * 4,
        scratch_shapes=[pltpu.VMEM((count, WIDTH, WIDTH), jnp.float32)] * 4
        + [pltpu.VMEM((BLOCK, count * BLOCK), jnp.float32)] * 3,
        compiler_params=pltpu.CompilerParams(vmem_limit_bytes=48 << 20),
    )(row_piece, col_piece, *packed)


def route_core():
    return ("row", [(r, r ^ 1) for r in range(8)])


def route_z(move):
    return ("row", [(z * 2 + k, move(z) * 2 + k) for z in range(4) for k in range(2)])


def route_x(move):
    return ("col", [(y * 4 + x, y * 4 + move(x)) for y in range(4) for x in range(4)])


def route_y(move):
    return ("col", [(y * 4 + x, move(y) * 4 + x) for y in range(4) for x in range(4)])


def send(array, route):
    return lax.ppermute(array, route[0], route[1])


def scatter_sum(slabs, route_of):
    arrived = [
        send(slabs[shift], route_of(lambda p, shift=shift: (p + shift) & 3)) for shift in (1, 3, 2)
    ]
    return slabs[0] + arrived[0] + arrived[1] + arrived[2]


def quad_levels(gram, route_of):
    one, three, two = (send(gram, route_of(lambda p, bit=bit: p ^ bit)) for bit in (1, 3, 2))
    pair = gram + one
    return pair, pair + (two + three)


def per_device(front, right_samples, left_samples):
    row_at, col_at = lax.axis_index("row"), lax.axis_index("col")
    place = jnp.stack([col_at >> 2, col_at & 3, row_at >> 1, row_at & 1]).astype(jnp.int32)

    along_x, along_y = row_product(front, right_samples, place)
    first = scatter_sum(along_x, route_x)
    second = scatter_sum(along_y, route_y)
    owned_rows = jnp.concatenate(
        [scatter_sum(first, route_y), scatter_sum(second, route_x)], axis=0
    )
    mine, other = col_product(front, left_samples, place)
    owned_cols = scatter_sum(mine + send(other, route_core()), route_z)

    row_piece = lax.all_to_all(owned_rows, "row", split_axis=0, concat_axis=0, tiled=True)
    col_piece = lax.all_to_all(owned_cols, "col", split_axis=0, concat_axis=0, tiled=True)

    gram = packed_gram(row_piece)
    nodes = [gram + send(gram, route_core())]
    for route_of in (route_z, route_x, route_y):
        nodes += quad_levels(nodes[-1], route_of)
    gram = packed_gram(col_piece)
    conodes = list(quad_levels(gram, route_x))
    conodes += quad_levels(conodes[-1], route_y)
    conodes.append(conodes[-1] + send(conodes[-1], route_core()))
    conodes += quad_levels(conodes[-1], route_z)

    row_basis, row_transfer, col_basis, col_transfer = finish_trees(
        row_piece, col_piece, nodes + conodes
    )
    return row_basis, row_transfer[None], col_basis, col_transfer[None]


def solution(mesh):
    in_specs = (P("row", "col"), P("col", None), P("row", None))
    out_specs = (
        P(("col", "row"), None),
        P(("col", "row"), None, None, None),
        P(("row", "col"), None),
        P(("row", "col"), None, None, None),
    )
    return jax.shard_map(
        per_device, mesh=mesh, in_specs=in_specs, out_specs=out_specs, check_vma=False
    )
```

```python
import functools

import jax
import jax.numpy as jnp
from jax import lax
from jax.experimental import pallas as pl
from jax.experimental.pallas import tpu as pltpu
from jax.sharding import PartitionSpec as P

WIDTH = 256
BLOCK = 64
HALF = 128
AHEAD = 2
BF = jnp.bfloat16


def dot(a, b, ca, cb, precision=None):
    return lax.dot_general(
        a, b, (((ca,), (cb,)), ((), ())), precision=precision, preferred_element_type=jnp.float32
    )


def split2(x):
    first = x.astype(BF)
    return first, (x - first.astype(jnp.float32)).astype(BF)


def split3(x):
    first = x.astype(BF)
    rest = x - first.astype(jnp.float32)
    second = rest.astype(BF)
    return first, second, (rest - second.astype(jnp.float32)).astype(BF)


def left6(parts, axis):
    a, b, c = parts
    return jnp.concatenate([a, a, a], axis=axis), jnp.concatenate([b, b, c], axis=axis)


def right6(parts, axis):
    a, b, c = parts
    return jnp.concatenate([a, b, c], axis=axis), jnp.concatenate([a, b, a], axis=axis)


def dot6(left, right, ca, cb):
    return dot(left[0], right[0], ca, cb) + dot(left[1], right[1], ca, cb)


def dot3(a, b, ca, cb):
    return dot(a[0], b[0], ca, cb) + (dot(a[0], b[1], ca, cb) + dot(a[1], b[0], ca, cb))


def row_kernel(place, f0, f1, f2, f3, samples, *refs):
    outs_x, outs_y = refs[:4], refs[4:8]
    coarse, fine, high, low = refs[8:]
    step = pl.program_id(0)

    @pl.when(step == 0)
    def _():
        coarse[...], fine[...] = split2(samples[...])

    for d, block in enumerate((f0, f1, f2, f3)):
        high[192 * d : 192 * (d + 1), :], low[192 * d : 192 * (d + 1), :] = split2(block[...])
    total = dot3((high[...], low[...]), (coarse[...], fine[...]), 1, 0)
    for d in range(4):
        outs_y[d][step] = total[192 * d + 96 : 192 * d + 192]

        @pl.when(step == d)
        def _(d=d):
            for e in range(4):
                outs_x[d][e] = total[192 * e : 192 * e + 96]


def row_product(front, samples, place):
    depth = front.shape[1]
    slab = jax.ShapeDtypeStruct((4, 96, WIDTH), jnp.float32)

    def block(d):
        return pl.BlockSpec(
            (192, depth), lambda i, place: (4 * ((place[0] + d) & 3) + ((place[1] + i) & 3), 0)
        )

    def whole(shape):
        return pl.BlockSpec(shape, lambda i, place: (0,) * len(shape))

    outs = pl.pallas_call(
        row_kernel,
        out_shape=[slab] * 8,
        grid_spec=pltpu.PrefetchScalarGridSpec(
            num_scalar_prefetch=1,
            grid=(4,),
            in_specs=[block(d) for d in range(4)] + [whole((depth, WIDTH))],
            out_specs=[whole(slab.shape)] * 8,
            scratch_shapes=[pltpu.VMEM((depth, WIDTH), BF)] * 2 + [pltpu.VMEM((768, depth), BF)] * 2,
        ),
        compiler_params=pltpu.CompilerParams(vmem_limit_bytes=40 << 20),
    )(place, front, front, front, front, samples)
    return outs[:4], outs[4:]


def col_kernel(place, front, samples, mine, other, total):
    step = pl.program_id(0)
    part = dot3(split2(front[...]), split2(samples[...]), 0, 0)

    @pl.when(step == 0)
    def _():
        total[...] = part

    @pl.when(step > 0)
    def _():
        total[...] += part

    @pl.when(step == pl.num_programs(0) - 1)
    def _():
        for d in range(4):
            base = 2 * ((place[2] + d) & 3)
            mine[d] = total[pl.ds(pl.multiple_of(192 * (base + place[3]), 192), 192), :]
            other[d] = total[pl.ds(pl.multiple_of(192 * (base + 1 - place[3]), 192), 192), :]


def col_product(front, samples, place):
    rows, depth = 768, front.shape[1]
    slab = jax.ShapeDtypeStruct((4, 192, WIDTH), jnp.float32)

    def whole(shape):
        return pl.BlockSpec(shape, lambda i, place: (0,) * len(shape))

    return pl.pallas_call(
        col_kernel,
        out_shape=[slab] * 2,
        grid_spec=pltpu.PrefetchScalarGridSpec(
            num_scalar_prefetch=1,
            grid=(front.shape[0] // rows,),
            in_specs=[
                pl.BlockSpec((rows, depth), lambda i, place: (i, 0)),
                pl.BlockSpec((rows, WIDTH), lambda i, place: (i, 0)),
            ],
            out_specs=[whole(slab.shape)] * 2,
            scratch_shapes=[pltpu.VMEM((depth, WIDTH), jnp.float32)],
        ),
        compiler_params=pltpu.CompilerParams(vmem_limit_bytes=40 << 20),
        cost_estimate=pl.CostEstimate(
            flops=6 * front.size * WIDTH, bytes_accessed=4 * front.size, transcendentals=0
        ),
    )(place, front, samples)


def gram_kernel(piece, packed):
    gram = dot(piece[...], piece[...], 0, 0, lax.Precision.HIGHEST)
    row = lax.broadcasted_iota(jnp.int32, (HALF, HALF), 0)
    col = lax.broadcasted_iota(jnp.int32, (HALF, HALF), 1)
    last = gram[HALF:, HALF:]
    packed[:HALF, :] = gram[:HALF, HALF:]
    packed[HALF:WIDTH, :] = jnp.where(row >= col, gram[:HALF, :HALF], last)
    diagonal = jnp.sum(jnp.where(row == col, last, 0.0), axis=0, keepdims=True)
    packed[WIDTH:, :] = jnp.broadcast_to(diagonal, (8, HALF))


def packed_gram(piece):
    vmem = pl.BlockSpec(memory_space=pltpu.VMEM)
    return pl.pallas_call(
        gram_kernel,
        out_shape=jax.ShapeDtypeStruct((WIDTH + 8, HALF), jnp.float32),
        in_specs=[vmem],
        out_specs=vmem,
    )(piece)


def unpack(packed, full):
    row = lax.broadcasted_iota(jnp.int32, (HALF, HALF), 0)
    col = lax.broadcasted_iota(jnp.int32, (HALF, HALF), 1)
    for b, source in enumerate(packed):
        mixed, across = source[HALF:WIDTH, :], source[:HALF, :]
        turned = mixed.T
        full[b, :HALF, HALF:] = across
        full[b, HALF:, :HALF] = across.T
        full[b, :HALF, :HALF] = jnp.where(row >= col, mixed, turned)
        diagonal = jnp.broadcast_to(source[WIDTH : WIDTH + 1, :], (HALF, HALF))
        full[b, HALF:, HALF:] = jnp.where(
            row == col, diagonal, jnp.where(row < col, mixed, turned)
        )


def factor_blocks(blocks, lower_out, upper_out):
    lanes = blocks.shape[1]
    sub = lax.broadcasted_iota(jnp.int32, (8, HALF), 0)
    lane = lax.broadcasted_iota(jnp.int32, (8, HALF), 1)
    seg = lane & (BLOCK - 1)
    base = lane - seg
    tiles = BLOCK // 8
    groups = lanes // HALF
    state = [
        [blocks[8 * t : 8 * t + 8, HALF * c : HALF * (c + 1)] for c in range(groups)]
        for t in range(tiles)
    ]

    def spread(c, k):
        return {
            t: jnp.take_along_axis(state[t][c], base + k, axis=1, mode="promise_in_bounds")
            for t in range(k // 8, tiles)
        }

    ahead = [{k: spread(c, k) for k in range(AHEAD)} for c in range(groups)]
    for k in range(BLOCK):
        top, inner = k // 8, k % 8
        at = seg == k
        for c in range(groups):
            row = state[top][c][inner : inner + 1, :]
            if k + AHEAD < BLOCK:
                ahead[c][k + AHEAD] = spread(c, k + AHEAD)
            column = ahead[c].pop(k)
            pivot = column[top][inner : inner + 1, :]
            scale = lax.rsqrt(pivot)
            square = scale * scale
            for m, later in ahead[c].items():
                weight = column[m // 8][m % 8 : m % 8 + 1, :] * square
                ahead[c][m] = {t: later[t] - column[t] * weight for t in later}
            done = jnp.where(at[:1], 1.0, row) * scale
            place = slice(HALF * c, HALF * (c + 1))
            lower_out[k : k + 1, place] = jnp.where(seg[:1] <= k, done, 0.0)
            upper_out[k : k + 1, place] = jnp.where(
                seg[:1] > k, done, jnp.where(at[:1], pivot * scale, 0.0)
            )
            scaled = done * scale
            for t in range(top, tiles):
                if t == top and inner == 7:
                    continue
                new = jnp.where(at, 0.0, state[t][c]) - column[t] * scaled
                state[t][c] = jnp.where(sub > inner, new, state[t][c]) if t == top else new


def factor_nodes(source, work, upper, inverse, blocks, lower_out, upper_out):
    count = source.shape[0]
    column = lax.broadcasted_iota(jnp.int32, (BLOCK, WIDTH), 1)
    row = lax.broadcasted_iota(jnp.int32, (BLOCK, WIDTH), 0)
    columns = lax.broadcasted_iota(jnp.int32, (WIDTH, WIDTH), 1)
    for j in range(WIDTH // BLOCK):
        src = source if j == 0 else work
        lo, hi = j * BLOCK, (j + 1) * BLOCK
        for b in range(count):
            blocks[:, b * BLOCK : (b + 1) * BLOCK] = src[b, lo:hi, lo:hi]
        factor_blocks(blocks, lower_out, upper_out)
        inside = (column >= lo) & (column < hi)
        unit = jnp.where(column - lo == row, 1.0, 0.0)
        for b in range(count):
            inv = lower_out[:, b * BLOCK : (b + 1) * BLOCK]
            line = jnp.where(inside, unit, src[b, lo:hi, :])
            rows = dot6(left6(split3(inv), 1), right6(split3(line), 0), 1, 0)
            upper[b, lo:hi, :] = jnp.where(column >= hi, rows, 0.0)
            inverse[b, lo:hi, :] = jnp.where(column < hi, rows, 0.0)
            upper[b, lo:hi, lo:hi] = upper_out[:, b * BLOCK : (b + 1) * BLOCK]
            if hi < WIDTH:
                parts = split3(rows)
                panel = tuple(p[:, hi:].T for p in parts)
                change = dot6(left6(panel, 1), right6(parts, 0), 1, 0)
                c = columns[hi:]
                kept = jnp.where((c >= lo) & (c < hi), 0.0, src[b, hi:, :])
                work[b, hi:, :] = kept - change


def tree_kernel(*refs, count):
    pieces, packed, outs = refs[:2], refs[2 : 2 + count], refs[2 + count : 6 + count]
    full, work, upper, inverse, blocks, lower_out, upper_out = refs[6 + count :]
    unpack(packed, full)
    factor_nodes(full, work, upper, inverse, blocks, lower_out, upper_out)
    levels = count // 2
    for side in range(2):
        basis, transfer = outs[2 * side : 2 * side + 2]
        leaf = side * levels
        basis[...] = dot3(split2(pieces[side][...]), split2(inverse[leaf]), 1, 1)
        for t in range(levels - 1):
            transfer[t] = dot3(split2(upper[leaf + t]), split2(inverse[leaf + t + 1]), 1, 1)


def finish_trees(row_piece, col_piece, packed):
    count = len(packed)
    basis = jax.ShapeDtypeStruct(row_piece.shape, jnp.float32)
    transfer = jax.ShapeDtypeStruct((count // 2 - 1, WIDTH, WIDTH), jnp.float32)
    vmem = pl.BlockSpec(memory_space=pltpu.VMEM)
    return pl.pallas_call(
        functools.partial(tree_kernel, count=count),
        out_shape=[basis, transfer, basis, transfer],
        in_specs=[vmem] * (2 + count),
        out_specs=[vmem] * 4,
        scratch_shapes=[pltpu.VMEM((count, WIDTH, WIDTH), jnp.float32)] * 4
        + [pltpu.VMEM((BLOCK, count * BLOCK), jnp.float32)] * 3,
        compiler_params=pltpu.CompilerParams(vmem_limit_bytes=48 << 20),
    )(row_piece, col_piece, *packed)


def route_core():
    return ("row", [(r, r ^ 1) for r in range(8)])


def route_z(move):
    return ("row", [(z * 2 + k, move(z) * 2 + k) for z in range(4) for k in range(2)])


def route_x(move):
    return ("col", [(y * 4 + x, y * 4 + move(x)) for y in range(4) for x in range(4)])


def route_y(move):
    return ("col", [(y * 4 + x, move(y) * 4 + x) for y in range(4) for x in range(4)])


def send(array, route):
    return lax.ppermute(array, route[0], route[1])


def scatter_sum(slabs, route_of):
    arrived = [
        send(slabs[shift], route_of(lambda p, shift=shift: (p + shift) & 3)) for shift in (1, 3, 2)
    ]
    return slabs[0] + arrived[0] + arrived[1] + arrived[2]


def quad_levels(gram, route_of):
    one, three, two = (send(gram, route_of(lambda p, bit=bit: p ^ bit)) for bit in (1, 3, 2))
    pair = gram + one
    return pair, pair + (two + three)


def per_device(front, right_samples, left_samples):
    row_at, col_at = lax.axis_index("row"), lax.axis_index("col")
    place = jnp.stack([col_at >> 2, col_at & 3, row_at >> 1, row_at & 1]).astype(jnp.int32)

    along_x, along_y = row_product(front, right_samples, place)
    first = scatter_sum(along_x, route_x)
    second = scatter_sum(along_y, route_y)
    owned_rows = jnp.concatenate(
        [scatter_sum(first, route_y), scatter_sum(second, route_x)], axis=0
    )
    mine, other = col_product(front, left_samples, place)
    owned_cols = scatter_sum(mine + send(other, route_core()), route_z)

    row_piece = lax.all_to_all(owned_rows, "row", split_axis=0, concat_axis=0, tiled=True)
    col_piece = lax.all_to_all(owned_cols, "col", split_axis=0, concat_axis=0, tiled=True)

    row_piece, col_piece = lax.optimization_barrier((row_piece, col_piece))
    gram = packed_gram(row_piece)
    nodes = [gram + send(gram, route_core())]
    for route_of in (route_z, route_x, route_y):
        nodes += quad_levels(nodes[-1], route_of)
    gram = packed_gram(col_piece)
    conodes = list(quad_levels(gram, route_x))
    conodes += quad_levels(conodes[-1], route_y)
    conodes.append(conodes[-1] + send(conodes[-1], route_core()))
    conodes += quad_levels(conodes[-1], route_z)

    row_basis, row_transfer, col_basis, col_transfer = finish_trees(
        row_piece, col_piece, nodes + conodes
    )
    return row_basis, row_transfer[None], col_basis, col_transfer[None]


def solution(mesh):
    in_specs = (P("row", "col"), P("col", None), P("row", None))
    out_specs = (
        P(("col", "row"), None),
        P(("col", "row"), None, None, None),
        P(("row", "col"), None),
        P(("row", "col"), None, None, None),
    )
    return jax.shard_map(
        per_device, mesh=mesh, in_specs=in_specs, out_specs=out_specs, check_vma=False
    )
```
